512 devices in a mesh: outer: 8 (over z_lo), shard: 64 (over y, x, z_hi, core).
Axes of the slice: x: 4, y: 4, z: 16 (z_hi: 2, z_lo: 8; z = z_hi * 8 + z_lo), core: 2. Of those that a mesh axis runs over, the one named last changes fastest.
Arguments:
- grads: bfloat16 [8, 64, 6144, 128], P('outer', 'shard'), may hold values from -0.3984375 to 0.3984375
- exponents: int32 [8, 6144], P('outer', 'shard'), may hold values from -10 to 0
- moment: float32 [6144, 128], P('shard'), may hold values from -2 to 2
- second: float32 [6144, 128], P('shard'), may hold values from 0.01 to 1
- master: float32 [6144, 128], P('shard'), may hold values from -6 to 6
Outputs:
- grad_total: float32 [6144, 128], P('shard')
- new_moment: float32 [6144, 128], P('shard')
- new_second: float32 [6144, 128], P('shard')
- new_master: float32 [6144, 128], P('shard')
- new_copy: bfloat16 [6144, 128], P('shard')
The draws below stay inside these ranges and needn't reach their ends.
All inputs are finite; a program needn't handle non-finite values.
Results may differ from the reference program's by a relative error of at most 0.014.
Values may be sent and summed in bfloat16 or wider, within the bound.
No kernel may reach another device: no remote copies, remote signals or barrier semaphores. Data moves between devices by JAX's collectives and lax.ppermute only.
A program may use at most 64 MiB of HBM per device.

```python
import math
import jax
import jax.numpy as jnp
from jax import lax

BLOCK = 128
ROWS = 6144
N_OUTER = 8
N_SHARD = 64


def touch_ends(result, rng, least, high):
    extent = result.shape
    place = [jax.random.randint(jax.random.fold_in(rng, axis), (), 0, extent[axis]) for axis in range(len(extent))]
    result = result.at[tuple(place)].set(least)
    longest = extent.index(max(extent))
    place[longest] = (place[longest] + 1) % extent[longest]
    return result.at[tuple(place)].set(high)


def strengthened(values, stream_key, source, target, parts, factor):
    def block_of(axis_at):
        return (jnp.arange(values.shape[axis_at]) // (values.shape[axis_at] // parts)).reshape((-1,) + (1,) * (values.ndim - 1 - axis_at))

    one_side = jax.random.permutation(stream_key, parts)[block_of(target)]
    far = (block_of(target) + parts // 2) % parts
    return jnp.where((block_of(source) == one_side) | (block_of(source) == far), factor * values, values)


def shard_levels(key, shape, shards, low, top_value):
    gain, own = 1.0, jax.random.fold_in(key, 6)
    for dim, blocks in shards:
        steps = jnp.exp(jax.random.uniform(jax.random.fold_in(own, dim), (blocks,), jnp.float32, low / len(shards), top_value / len(shards)))
        gain = gain * jnp.repeat(steps, shape[dim] // blocks).reshape([-1 if axis == dim else 1 for axis in range(len(shape))])
    return gain


def noise(key, extent, deviation, most, split=(), kind=jnp.bfloat16):
    result = jax.random.normal(key, extent, jnp.float32) * deviation
    if len(split) > 0:
        result = shard_levels(key, extent, split, -0.22, 0.18) * result
    return jnp.clip(result, min=-most, max=most).astype(kind)


def heavy_noise(stream_key, dims, width, reach, cuts, heavy, held_as=jnp.bfloat16):
    drawn = width * jax.random.normal(stream_key, dims, jnp.float32)
    if cuts:
        drawn = drawn * shard_levels(stream_key, dims, cuts, -0.22, 0.18)
    return jnp.clip(strengthened(drawn, jax.random.fold_in(stream_key, 3), *heavy), -reach, reach).astype(held_as)


def setup_inputs(seed: int = 0) -> dict:
    key_list = jax.random.split(jax.random.key(seed), 6)
    grads = heavy_noise(key_list[0], (N_OUTER, N_SHARD, ROWS, BLOCK), 0.05, 0.3984375, ((0, 8), (1, 64)), (1, 2, 64, 4.0))
    exponents = touch_ends(jax.random.randint(key_list[1], (N_OUTER, ROWS), -10, 1), jax.random.fold_in(key_list[1], 1), -10, 0).astype(jnp.int32)
    moment = noise(key_list[2], (ROWS, BLOCK), 0.3, 2.0, ((0, 64),), jnp.float32)
    second = jnp.clip(jnp.exp(math.log(1.0) - 4.6051702 * jax.random.uniform(key_list[3], (ROWS, BLOCK), jnp.float32) ** shard_levels(key_list[3], (ROWS, BLOCK), ((0, 64),), -0.2, 0.2)), 0.01, 1.0)
    master = noise(key_list[4], (ROWS, BLOCK), 1.0, 6.0, ((0, 64),), jnp.float32)
    return dict(grads=grads, exponents=exponents, moment=moment, second=second, master=master)


def hadamard(length):
    positions = jnp.arange(length, dtype=jnp.int32)
    intersection = jnp.bitwise_and(positions[:, None], positions[None, :])
    parity = jnp.zeros((length, length), jnp.int32)
    for bit_place in range(length.bit_length() - 1):
        parity = parity + jnp.bitwise_and(jnp.right_shift(intersection, bit_place), 1)
    signs = 1 - 2 * jnp.bitwise_and(parity, 1)
    return signs.astype(jnp.float32) / math.sqrt(length)

def quantize_restore(group_rows, scale_exps, transform):
    rotated = jnp.dot(group_rows, transform, precision=lax.Precision.HIGHEST, preferred_element_type=jnp.float32)
    powers = jnp.exp2(scale_exps.astype(jnp.float32))[:, None]
    quantized = jnp.clip((rotated / powers).astype(jnp.bfloat16), -448.0, 448.0)
    quantized = lax.optimization_barrier(quantized)
    return quantized.astype(jnp.float32) * powers

def adam_update(gradient, moment, second, master):
    new_moment = 0.9 * moment + 0.1 * gradient
    new_second = 0.95 * second + 0.05 * gradient * gradient
    direction = new_moment / (1.0 - 0.9 ** 10) / (jnp.sqrt(new_second / (1.0 - 0.95 ** 10)) + 1e-08)
    new_master = master - 0.01 * (direction + 0.1 * master)
    return (new_moment, new_second, new_master)

def reference(grads, exponents, moment, second, master):
    transform = hadamard(BLOCK)

    def per_group(pair):
        group_grads, scale_exps = pair
        group_rows = lax.optimization_barrier(jnp.sum(group_grads.astype(jnp.float32), axis=0))
        return quantize_restore(group_rows, scale_exps, transform)
    restored = lax.map(per_group, (grads, exponents))
    summed = lax.optimization_barrier(jnp.sum(restored, axis=0))
    grad_total = jnp.dot(summed, transform, precision=lax.Precision.HIGHEST, preferred_element_type=jnp.float32)
    new_moment, new_second, new_master = adam_update(grad_total, moment, second, master)
    return (grad_total, new_moment, new_second, new_master, new_master.astype(jnp.bfloat16))
```

```python
import math

import jax
import jax.numpy as jnp
import numpy as np
from jax import lax
from jax.sharding import Mesh, PartitionSpec as P

OUTER, Y, X, HALF, CORE = "outer", "y", "x", "half", "core"
SHARD = (Y, X, HALF, CORE)


def signs(length):
    positions = np.arange(length)
    parity = np.array([bin(v).count("1") & 1 for v in range(length)])
    return (1 - 2 * parity[positions[:, None] & positions[None, :]]).astype(np.float32)


def rotate(rows, sign_matrix):
    head = rows.astype(jnp.bfloat16)
    tail = (rows - head.astype(jnp.float32)).astype(jnp.bfloat16)
    both = jnp.concatenate([head, tail], axis=1)
    out = jnp.dot(both, jnp.concatenate([sign_matrix, sign_matrix], axis=0), preferred_element_type=jnp.float32)
    return out * (1.0 / math.sqrt(sign_matrix.shape[0]))


def adam_update(gradient, moment, second, master):
    new_moment = 0.9 * moment + 0.1 * gradient
    new_second = 0.95 * second + 0.05 * gradient * gradient
    direction = new_moment / (1.0 - 0.9**10) / (jnp.sqrt(new_second / (1.0 - 0.95**10)) + 1e-08)
    new_master = master - 0.01 * (direction + 0.1 * master)
    return (new_moment, new_second, new_master)


def per_device(grads, exponents, moment, second, master):
    rows, block = moment.shape
    sign_matrix = jnp.asarray(signs(block), jnp.bfloat16)
    parts = grads.reshape(16, 2, 2, rows, block)
    core = lax.axis_index(CORE)
    half = lax.axis_index(HALF)

    with jax.named_scope("core_exchange"):
        away = lax.dynamic_index_in_dim(parts, 1 - core, 2, keepdims=False)
        kept = lax.dynamic_index_in_dim(parts, core, 2, keepdims=False)
        came = lax.ppermute(away, CORE, [(0, 1), (1, 0)])
        chip = (kept.astype(jnp.float32) + came.astype(jnp.float32)).astype(jnp.bfloat16)

    with jax.named_scope("plane_exchange"):
        plane = lax.all_to_all(chip.reshape(16, 2 * rows, block), (Y, X), 0, 0, tiled=True)
        partial = jnp.sum(plane.astype(jnp.float32), axis=0)
        rotated = rotate(partial, sign_matrix).astype(jnp.bfloat16).reshape(2, 1, rows, block)

    with jax.named_scope("z_exchange"):
        scales = jnp.pad(exponents.astype(jnp.bfloat16), ((0, 7), (0, block - rows)))
        scales = jnp.broadcast_to(scales[None, None], (2, 1, 8, block))
        packet = jnp.concatenate([rotated, scales], axis=2)
        packet = jnp.broadcast_to(packet, (2, 8, rows + 8, block)).reshape(16, rows + 8, block)
        arrived = lax.all_to_all(packet, (HALF, OUTER), 0, 0, tiled=True).reshape(2, 8, rows + 8, block)

    with jax.named_scope("quantize"):
        group = arrived[0, :, :rows].astype(jnp.float32) + arrived[1, :, :rows].astype(jnp.float32)
        exps = lax.dynamic_index_in_dim(arrived[:, :, rows, :rows], half, 0, keepdims=False).astype(jnp.float32)
        down, up = jnp.exp2(-exps)[:, :, None], jnp.exp2(exps)[:, :, None]
        quantized = jnp.clip((group * down).astype(jnp.bfloat16), -448.0, 448.0)
        summed = jnp.sum(quantized.astype(jnp.float32) * up, axis=0)

    with jax.named_scope("adam"):
        grad_total = rotate(summed, sign_matrix)
        new_moment, new_second, new_master = adam_update(grad_total, moment, second, master)
    return (grad_total, new_moment, new_second, new_master, new_master.astype(jnp.bfloat16))


def solution(mesh):
    fine = Mesh(mesh.devices.reshape(8, 4, 4, 2, 2), (OUTER,) + SHARD)
    owner = P(SHARD, None)
    return jax.shard_map(
        per_device,
        mesh=fine,
        in_specs=(P(OUTER, SHARD, None, None), P(OUTER, SHARD), owner, owner, owner),
        out_specs=(owner,) * 5,
        check_vma=False,
    )
```

```python
import math

import jax
import jax.numpy as jnp
import numpy as np
from jax import lax
from jax.sharding import Mesh, PartitionSpec as P

PAIR, SIDE, Y, X, HALF, CORE = "pair", "side", "y", "x", "half", "core"
OUTER, SHARD = (PAIR, SIDE), (Y, X, HALF, CORE)
SWAP = [(0, 1), (1, 0)]


def signs(length):
    positions = np.arange(length)
    parity = np.array([bin(v).count("1") & 1 for v in range(length)])
    return (1 - 2 * parity[positions[:, None] & positions[None, :]]).astype(np.float32)


def rotate(rows, sign_matrix):
    head = rows.astype(jnp.bfloat16)
    tail = (rows - head.astype(jnp.float32)).astype(jnp.bfloat16)
    both = jnp.concatenate([head, tail], axis=1)
    out = jnp.dot(both, jnp.concatenate([sign_matrix, sign_matrix], axis=0), preferred_element_type=jnp.float32)
    return out * (1.0 / math.sqrt(sign_matrix.shape[0]))


def adam_update(gradient, moment, second, master):
    new_moment = 0.9 * moment + 0.1 * gradient
    new_second = 0.95 * second + 0.05 * gradient * gradient
    direction = new_moment / (1.0 - 0.9**10) / (jnp.sqrt(new_second / (1.0 - 0.95**10)) + 1e-08)
    new_master = master - 0.01 * (direction + 0.1 * master)
    return (new_moment, new_second, new_master)


def per_device(grads, exponents, moment, second, master):
    rows, block = moment.shape
    part = rows // 2
    sign_matrix = jnp.asarray(signs(block), jnp.bfloat16)
    parts = grads.reshape(16, 2, 2, rows, block)
    core, half, side = lax.axis_index(CORE), lax.axis_index(HALF), lax.axis_index(SIDE)

    with jax.named_scope("limits"):
        bound = (448.0 * jnp.exp2(exponents.astype(jnp.float32))).astype(jnp.bfloat16).reshape(2, 1, part)
        bound = jnp.pad(bound, ((0, 0), (0, 7), (0, block - part)))
        mine = lax.broadcasted_iota(jnp.int32, (2, 1, 1, 1), 0) == half
        bounds = jnp.where(mine, bound[None], 0.0)
        first = side == 0

    with jax.named_scope("core_exchange"):
        away = lax.dynamic_index_in_dim(parts, 1 - core, 2, keepdims=False)
        kept = lax.dynamic_index_in_dim(parts, core, 2, keepdims=False)
        came = lax.ppermute(away, CORE, SWAP)
        chip = (kept.astype(jnp.float32) + came.astype(jnp.float32)).astype(jnp.bfloat16)
        chip, bounds = lax.optimization_barrier((chip, bounds))

    with jax.named_scope("plane_exchange"):
        plane = lax.all_to_all(chip.reshape(4, 4, 2 * rows, block).transpose(1, 0, 2, 3).reshape(16, 2 * rows, block), (X, Y), 0, 0, tiled=True)
        partial = jnp.sum(plane.astype(jnp.float32), axis=0)
        rotated = rotate(partial, sign_matrix).astype(jnp.bfloat16).reshape(2, 2, part, block)

    with jax.named_scope("z_exchange"):
        packet = jnp.concatenate([rotated, bounds], axis=2)[:, None]
        packet = jnp.broadcast_to(packet, (2, 4, 2, part + 8, block)).reshape(16, part + 8, block)
        packet = lax.optimization_barrier(packet)
        arrived = lax.all_to_all(packet, (HALF, PAIR, SIDE), 0, 0, tiled=True).reshape(2, 8, part + 8, block)

    with jax.named_scope("quantize"):
        both = arrived[0].astype(jnp.float32) + arrived[1].astype(jnp.float32)
        group, limit = both[:, :part], both[:, part, :part, None]
        restored = jnp.clip(group.astype(jnp.bfloat16).astype(jnp.float32), -limit, limit)
        summed = rotate(jnp.sum(restored, axis=0), sign_matrix)

    with jax.named_scope("pair_exchange"):
        other = lax.ppermute(summed, SIDE, SWAP)
        grad_total = jnp.concatenate([jnp.where(first, summed, other), jnp.where(first, other, summed)], axis=0)

    with jax.named_scope("adam"):
        new_moment, new_second, new_master = adam_update(grad_total, moment, second, master)
    return (grad_total, new_moment, new_second, new_master, new_master.astype(jnp.bfloat16))


def solution(mesh):
    fine = Mesh(mesh.devices.reshape(4, 2, 4, 4, 2, 2), OUTER + SHARD)
    owner = P(SHARD, None)
    return jax.shard_map(
        per_device,
        mesh=fine,
        in_specs=(P(OUTER, SHARD, None, None), P(OUTER, SHARD), owner, owner, owner),
        out_specs=(owner,) * 5,
        check_vma=False,
    )
```

```python
import math

import jax
import jax.numpy as jnp
import numpy as np
from jax import lax
from jax.sharding import Mesh, PartitionSpec as P

RUN, SIDE, PLANE, HALF, CORE = "run", "side", "plane", "half", "core"
OUTER, SHARD = (RUN, SIDE), (PLANE, HALF, CORE)
SIZES = {RUN: 2, SIDE: 4, PLANE: 16, HALF: 2, CORE: 2}

PLANE_ORDER = [4 * y + x for x in (3, 2, 1, 0) for y in (3, 2, 1, 0)]
Z_ORDER = [11, 10, 9, 8, 15, 14, 13, 12, 7, 6, 5, 4, 3, 2, 1, 0]
SIDE_ORDER = [3, 2, 1, 0]


def exchange(packets, axes, order):
    sent = lax.optimization_barrier(jnp.stack([packets[k] for k in order]))
    came = lax.all_to_all(sent, axes, 0, 0, tiled=True, axis_index_groups=[order])
    return [came[order.index(k)] for k in range(len(order))]


def signs(length):
    positions = np.arange(length)
    parity = np.array([bin(v).count("1") & 1 for v in range(length)])
    return (1 - 2 * parity[positions[:, None] & positions[None, :]]).astype(np.float32)


def rotate(rows, sign_matrix):
    head = rows.astype(jnp.bfloat16)
    tail = (rows - head.astype(jnp.float32)).astype(jnp.bfloat16)
    both = jnp.concatenate([head, tail], axis=1)
    out = jnp.dot(both, jnp.concatenate([sign_matrix, sign_matrix], axis=0), preferred_element_type=jnp.float32)
    return out * (1.0 / math.sqrt(sign_matrix.shape[0]))


def adam_update(gradient, moment, second, master):
    new_moment = 0.9 * moment + 0.1 * gradient
    new_second = 0.95 * second + 0.05 * gradient * gradient
    direction = new_moment / (1.0 - 0.9**10) / (jnp.sqrt(new_second / (1.0 - 0.95**10)) + 1e-08)
    new_master = master - 0.01 * (direction + 0.1 * master)
    return (new_moment, new_second, new_master)


def per_device(grads, exponents, moment, second, master):
    rows, block = moment.shape
    sides, n_outer = SIZES[SIDE], SIZES[RUN] * SIZES[SIDE]
    part = rows // sides
    sign_matrix = jnp.asarray(signs(block), jnp.bfloat16)
    parts = grads.reshape(SIZES[PLANE], 2, 2, rows, block)
    core, half = lax.axis_index(CORE), lax.axis_index(HALF)

    with jax.named_scope("limits"):
        bound = (448.0 * jnp.exp2(exponents.astype(jnp.float32))).astype(jnp.bfloat16).reshape(sides, 1, part)
        bound = jnp.pad(bound, ((0, 0), (0, 7), (0, block - part)))
        mine = lax.broadcasted_iota(jnp.int32, (2, 1, 1, 1), 0) == half
        bounds = jnp.where(mine, bound[None], 0.0)

    with jax.named_scope("core_exchange"):
        away = lax.dynamic_index_in_dim(parts, 1 - core, 2, keepdims=False)
        kept = lax.dynamic_index_in_dim(parts, core, 2, keepdims=False)
        came = lax.ppermute(away, CORE, [(0, 1), (1, 0)])
        chip = (kept.astype(jnp.float32) + came.astype(jnp.float32)).astype(jnp.bfloat16)
        chip, bounds = lax.optimization_barrier((chip.reshape(SIZES[PLANE], 2 * rows, block), bounds))

    with jax.named_scope("plane_exchange"):
        partial = sum(piece.astype(jnp.float32) for piece in exchange(chip, PLANE, PLANE_ORDER))
        rotated = rotate(partial, sign_matrix).astype(jnp.bfloat16).reshape(2, sides, part, block)

    with jax.named_scope("z_exchange"):
        packet = jnp.concatenate([rotated, bounds], axis=2)
        packets = [packet[z // n_outer, z % sides] for z in range(2 * n_outer)]
        arrived = exchange(packets, (HALF, RUN, SIDE), Z_ORDER)

    with jax.named_scope("quantize"):
        total = jnp.zeros((part, block), jnp.float32)
        for o in range(n_outer):
            both = arrived[o].astype(jnp.float32) + arrived[n_outer + o].astype(jnp.float32)
            limit = both[part, :part, None]
            total += jnp.clip(both[:part].astype(jnp.bfloat16).astype(jnp.float32), -limit, limit)

    with jax.named_scope("quad_exchange"):
        summed = jnp.concatenate(exchange([total] * sides, SIDE, SIDE_ORDER), axis=0)
        grad_total = rotate(summed, sign_matrix)

    with jax.named_scope("adam"):
        new_moment, new_second, new_master = adam_update(grad_total, moment, second, master)
    return (grad_total, new_moment, new_second, new_master, new_master.astype(jnp.bfloat16))


def solution(mesh):
    fine = Mesh(mesh.devices.reshape([SIZES[a] for a in OUTER + SHARD]), OUTER + SHARD)
    owner = P(SHARD, None)
    return jax.shard_map(
        per_device,
        mesh=fine,
        in_specs=(P(OUTER, SHARD, None, None), P(OUTER, SHARD), owner, owner, owner),
        out_specs=(owner,) * 5,
        check_vma=False,
    )
```

```python
import math

import jax
import jax.numpy as jnp
import numpy as np
from jax import lax
from jax.sharding import Mesh, PartitionSpec as P

RUN, SIDE, PLANE, HALF, CORE = "run", "side", "plane", "half", "core"
OUTER, SHARD = (RUN, SIDE), (PLANE, HALF, CORE)
SIZES = {RUN: 2, SIDE: 4, PLANE: 16, HALF: 2, CORE: 2}

PLANE_ORDER = [4 * y + x for x in (3, 2, 1, 0) for y in (3, 2, 1, 0)]
Z_ORDER = [11, 10, 9, 8, 15, 14, 13, 12, 7, 6, 5, 4, 3, 2, 1, 0]
SIDE_ORDER = [3, 2, 1, 0]


def exchange(packets, axes, order):
    sent = lax.optimization_barrier(jnp.stack([packets[k] for k in order]))
    came = lax.all_to_all(sent, axes, 0, 0, tiled=True, axis_index_groups=[order])
    return [came[order.index(k)] for k in range(len(order))]


def signs(length):
    positions = np.arange(length)
    parity = np.array([bin(v).count("1") & 1 for v in range(length)])
    return (1 - 2 * parity[positions[:, None] & positions[None, :]]).astype(np.float32)


def rotate(rows, sign_matrix):
    head = lax.reduce_precision(rows, 8, 7)
    both = jnp.concatenate([head, rows - head], axis=1).astype(jnp.bfloat16)
    out = jnp.dot(both, jnp.concatenate([sign_matrix, sign_matrix], axis=0), preferred_element_type=jnp.float32)
    return out * (1.0 / math.sqrt(sign_matrix.shape[0]))


def adam_update(gradient, moment, second, master):
    new_moment = 0.9 * moment + 0.1 * gradient
    new_second = 0.95 * second + 0.05 * gradient * gradient
    direction = new_moment / (1.0 - 0.9**10) / (jnp.sqrt(new_second / (1.0 - 0.95**10)) + 1e-08)
    new_master = master - 0.01 * (direction + 0.1 * master)
    return (new_moment, new_second, new_master)


def per_device(grads, exponents, moment, second, master):
    rows, block = moment.shape
    sides, n_outer = SIZES[SIDE], SIZES[RUN] * SIZES[SIDE]
    part = rows // sides
    sign_matrix = jnp.asarray(signs(block), jnp.bfloat16)
    parts = grads.reshape(SIZES[PLANE], 2, 2, rows, block)
    core, half = lax.axis_index(CORE), lax.axis_index(HALF)

    with jax.named_scope("limits"):
        bound = (448.0 * jnp.exp2(exponents.astype(jnp.float32))).astype(jnp.bfloat16).reshape(sides, 1, part)
        bound = jnp.pad(bound, ((0, 0), (0, 7), (0, block - part)))
        mine = lax.broadcasted_iota(jnp.int32, (2, 1, 1, 1), 0) == half
        bounds = jnp.where(mine, bound[None], 0.0)

    with jax.named_scope("core_exchange"):
        away = lax.dynamic_index_in_dim(parts, 1 - core, 2, keepdims=False)
        kept = lax.dynamic_index_in_dim(parts, core, 2, keepdims=False)
        came = lax.ppermute(away, CORE, [(0, 1), (1, 0)])
        chip = (kept.astype(jnp.float32) + came.astype(jnp.float32)).astype(jnp.bfloat16)
        chip, bounds = lax.optimization_barrier((chip.reshape(SIZES[PLANE], 2 * rows, block), bounds))

    with jax.named_scope("plane_exchange"):
        partial = sum(piece.astype(jnp.float32) for piece in exchange(chip, PLANE, PLANE_ORDER))
        rotated = rotate(partial, sign_matrix).astype(jnp.bfloat16).reshape(2, sides, part, block)

    with jax.named_scope("z_exchange"):
        packet = jnp.concatenate([rotated, bounds], axis=2)
        packets = [packet[z // n_outer, z % sides] for z in range(2 * n_outer)]
        arrived = exchange(packets, (HALF, RUN, SIDE), Z_ORDER)

    with jax.named_scope("quantize"):
        total = jnp.zeros((part, block), jnp.float32)
        for o in range(n_outer):
            both = arrived[o].astype(jnp.float32) + arrived[n_outer + o].astype(jnp.float32)
            limit = both[part, :part, None]
            total += jnp.clip(lax.reduce_precision(both[:part], 8, 7), -limit, limit)

    with jax.named_scope("quad_exchange"):
        summed = jnp.concatenate(exchange([total] * sides, SIDE, SIDE_ORDER), axis=0)
        grad_total = rotate(summed, sign_matrix)

    with jax.named_scope("adam"):
        new_moment, new_second, new_master = adam_update(grad_total, moment, second, master)
    return (grad_total, new_moment, new_second, new_master, new_master.astype(jnp.bfloat16))


def solution(mesh):
    fine = Mesh(mesh.devices.reshape([SIZES[a] for a in OUTER + SHARD]), OUTER + SHARD)
    owner = P(SHARD, None)
    return jax.shard_map(
        per_device,
        mesh=fine,
        in_specs=(P(OUTER, SHARD, None, None), P(OUTER, SHARD), owner, owner, owner),
        out_specs=(owner,) * 5,
        check_vma=False,
    )
```
